32 devices in a mesh: groups: 2 (over y), dp: 4 (over z), fsdp: 4 (over x, core).
Axes of the slice: x: 2, y: 2, z: 4, core: 2. Of those that a mesh axis runs over, the one named last changes fastest.
Arguments:
- hidden: bfloat16 [4096, 5120], P(('groups', 'dp', 'fsdp')), parts along dimension 0, may hold values from -160 to 160
- queries: bfloat16 [4096, 2560], P(('groups', 'dp', 'fsdp')), parts along dimension 0, may hold values from -6 to 6
- source_table: bfloat16 [8, 5120], replicated, may hold values from -6 to 6
- norm_gain: float32 [5120], replicated, may hold values from 0.25 to 1.75
- key_value_weight: bfloat16 [5120, 1024], P(None, 'fsdp'), may hold values from -0.078125 to 0.078125
- value_projection_bias: float32 [512], replicated, may hold values from -3 to 3
- seq_lengths: int32 [8, 16], P(('groups', 'fsdp')), parts along dimension 0, may hold values from 1 to 32, as said below
- seq_sources: int32 [8, 16], P(('groups', 'fsdp')), parts along dimension 0, may hold values from 0 to 7
- dest_device: int32 [8, 16], P(('groups', 'fsdp')), parts along dimension 0, may hold values from 0 to 3, as said below
- dest_slot: int32 [8, 16], P(('groups', 'fsdp')), parts along dimension 0, may hold values from 0 to 96, as said below
- segment_ids: int32 [4096], P(('groups', 'dp', 'fsdp')), parts along dimension 0, may hold values from -1 to 127, as said below
Outputs:
- attention_out: bfloat16 [4096, 2560], P(('groups', 'dp', 'fsdp')), parts along dimension 0
The draws below stay inside these ranges and needn't reach their ends.
There are 2 independent parts, one for each index of `groups`. The reference program is written for one: setup_inputs(seed, part) draws one part's arguments, and reference() takes and returns one part's arrays. A program takes and returns all parts, laid end to end along the dimension named above; an argument that names none is the same for every part. Nothing has to cross between parts.
Inputs may be any that keep to these rules, and one draw needn't show every extreme that they name: `seq_lengths`: the 4 slots of a block are packed from its first row in slot order; in every fsdp index there is one dp index all of whose received sequences have length 32. `dest_device`: each receiving block gets 4 sequences. `dest_slot`: the sequences sent to one block fill its first rows without gaps or intersections; in every fsdp index one receiving block is filled completely. `segment_ids`: -1 exactly on rows that receive nothing, which come last in a block; over a block's filled rows ids never fall, the last filled row has id 128 - 1, and a document lies within one sequence.
All inputs are finite; a program needn't handle non-finite values.
Results may differ from the reference program's by a relative error of at most 0.0056.
Values may be sent and summed in bfloat16 or wider, within the bound.
A program may use at most 64 MiB of HBM per device.

```python
import math
import jax
import jax.numpy as jnp
from jax import lax

MODEL_WIDTH = 5120
HEAD_SIZE = 128
QUERY_HEADS = 20
KEY_VALUE_HEADS = 4
SOURCES = 8
SEQS = 4
DEVICE_TOKENS = 128
MOST = 32
TOKENS = 2048
N_DP = 4
N_FSDP = 4


doc_break = 8


def column_plan(key):
    key_rows = jax.random.split(key, 5)
    count = N_DP * SEQS
    lengths = jax.random.randint(key_rows[0], (count,), 1, MOST + 1)
    forced = jax.random.randint(key_rows[1], (), 0, N_DP)
    lengths = jnp.where(jnp.arange(count) // SEQS == forced, MOST, lengths).astype(jnp.int32)
    grid = lengths.reshape(N_DP, SEQS)
    offsets = (jnp.cumsum(grid, axis=1) - grid).reshape(-1).astype(jnp.int32)
    targets = (jnp.arange(count) // SEQS).astype(jnp.int32)
    order = jax.random.permutation(key_rows[2], count)
    src_lengths = jnp.zeros((count,), jnp.int32).at[order].set(lengths)
    src_targets = jnp.zeros((count,), jnp.int32).at[order].set(targets)
    src_offsets = jnp.zeros((count,), jnp.int32).at[order].set(offsets)
    tags = jax.random.randint(key_rows[3], (count,), 0, SOURCES).astype(jnp.int32)
    places = jnp.arange(DEVICE_TOKENS)
    starts = jnp.any(places[None, :, None] == offsets.reshape(N_DP, SEQS)[:, None, :], axis=2)
    breaks = jax.random.randint(key_rows[4], (N_DP, DEVICE_TOKENS), 0, doc_break) == 0
    alive_mask = places[None, :] < jnp.sum(grid, axis=1)[:, None]
    flags = ((starts | breaks) & alive_mask).astype(jnp.int32)
    docs = jnp.sum(flags, axis=1, keepdims=True)
    segments = jnp.where(alive_mask, jnp.cumsum(flags, axis=1) - 1 + DEVICE_TOKENS - docs, -1).astype(jnp.int32)
    return (src_lengths, tags, src_targets, src_offsets, segments)


def full_plan(key):
    return jax.vmap(column_plan)(jax.random.split(key, N_FSDP))


def draw_seq_lengths(key, part):
    shared = full_plan(key)
    return shared[0]


def draw_seq_sources(key, part):
    shared = full_plan(key)
    return shared[1]


def draw_dest_device(key, part):
    shared = full_plan(key)
    return shared[2]


def draw_dest_slot(key, part):
    shared = full_plan(key)
    return shared[3]


def draw_segment_ids(key, part):
    shared = full_plan(key)
    return jnp.transpose(shared[4].reshape(N_FSDP, N_DP, DEVICE_TOKENS), (1, 0, 2)).reshape(-1)


def draw_hidden(key, part):
    key = jax.random.fold_in(key, 11)
    key_rows = jax.random.split(key, 3)
    columns = jnp.exp(jax.random.uniform(key_rows[1], (1, MODEL_WIDTH), jnp.float32, math.log(0.5), math.log(2.0)))
    row_scale = jnp.exp(jax.random.uniform(key_rows[0], (TOKENS, 1), jnp.float32, 0.0, math.log(10.0)))
    base = jnp.clip(jax.random.normal(key_rows[2], (TOKENS, MODEL_WIDTH), jnp.float32), -6.0, 6.0)
    return (base * row_scale * columns).astype(jnp.bfloat16)


def steps_of(stream_key, extent, shards, low, top_value):
    level, own = 1.0, jax.random.fold_in(stream_key, 6)
    for axis_at, shards_of in shards:
        draws = jnp.exp(jax.random.uniform(jax.random.fold_in(own, axis_at), (shards_of,), jnp.float32, low / len(shards), top_value / len(shards)))
        level = level * jnp.repeat(draws, extent[axis_at] // shards_of).reshape([-1 if axis == axis_at else 1 for axis in range(len(extent))])
    return level


def bell_draw(own_key, dims, width, bound, cuts=(), kind=jnp.bfloat16):
    factor_of = steps_of(own_key, dims, cuts, -0.22, 0.18) if cuts else 1.0
    array = jax.random.normal(own_key, dims, jnp.float32) * width * factor_of
    return jnp.minimum(jnp.maximum(array, -bound), bound).astype(kind)


def setup_inputs(seed: int = 0, part: int = 0) -> dict:
    key_of = jax.random.split(jax.random.key(seed), 12)
    part_splits = jax.random.split(jax.random.fold_in(key_of[11], part), 12)
    return {
        "hidden": draw_hidden(jax.random.fold_in(jax.random.fold_in(key_of[11], part), 71), part),
        "queries": bell_draw(part_splits[1], (TOKENS, QUERY_HEADS * HEAD_SIZE), 1.0, 6.0, ((0, 16),)),
        "source_table": bell_draw(key_of[2], (SOURCES, MODEL_WIDTH), 1.0, 6.0),
        "norm_gain": jnp.clip(1.0 + 0.15 * jax.random.normal(key_of[3], (MODEL_WIDTH,), jnp.float32), 0.25, 1.75),
        "key_value_weight": bell_draw(key_of[4], (MODEL_WIDTH, 2 * KEY_VALUE_HEADS * HEAD_SIZE), MODEL_WIDTH ** -0.5, 0.078125, ((1, 4),)),
        "value_projection_bias": bell_draw(key_of[5], (KEY_VALUE_HEADS * HEAD_SIZE,), 0.5, 3.0, (), jnp.float32),
        "seq_lengths": draw_seq_lengths(jax.random.fold_in(jax.random.fold_in(key_of[11], part), 71), part),
        "seq_sources": draw_seq_sources(jax.random.fold_in(jax.random.fold_in(key_of[11], part), 71), part),
        "dest_device": draw_dest_device(jax.random.fold_in(jax.random.fold_in(key_of[11], part), 71), part),
        "dest_slot": draw_dest_slot(jax.random.fold_in(jax.random.fold_in(key_of[11], part), 71), part),
        "segment_ids": draw_segment_ids(jax.random.fold_in(jax.random.fold_in(key_of[11], part), 71), part),
    }


epsilon = 1e-06

def source_rows(lengths, targets, offsets, input_rows):
    devices = lengths.shape[0] // SEQS
    grid = lengths.reshape(devices, SEQS)
    starts = (jnp.cumsum(grid, axis=1) - grid).reshape(-1).astype(jnp.int32)
    owners = (jnp.arange(devices * SEQS) // SEQS).astype(jnp.int32)
    src_base = owners * input_rows + starts
    dst_base = targets * input_rows + offsets
    places = jnp.arange(devices * input_rows).astype(jnp.int32)
    inside = (places[:, None] >= dst_base[None, :]) & (places[:, None] < (dst_base + lengths)[None, :])
    shifts = lax.optimization_barrier(jnp.sum(jnp.where(inside, (src_base - dst_base)[None, :], 0), axis=1)).astype(jnp.int32)
    alive_mask = jnp.any(inside, axis=1)
    return (jnp.where(alive_mask, places + shifts, 0).astype(jnp.int32), alive_mask)

def normalize(hidden_rows, table, gain, lengths, tags):
    input_rows = hidden_rows.shape[0]
    starts = (jnp.cumsum(lengths) - lengths).astype(jnp.int32)
    places = jnp.arange(input_rows).astype(jnp.int32)
    inside = (places[:, None] >= starts[None, :]) & (places[:, None] < (starts + lengths)[None, :])
    kinds = jnp.arange(SOURCES).astype(jnp.int32)
    picks = jnp.any(inside[:, :, None] & (tags[None, :, None] == kinds[None, None, :]), axis=1)
    summed = hidden_rows.astype(jnp.float32) + jnp.dot(picks.astype(table.dtype), table, preferred_element_type=jnp.float32)
    scale = lax.rsqrt(lax.optimization_barrier(jnp.mean(summed * summed, axis=1, keepdims=True)) + epsilon)
    return (summed * scale * gain).astype(hidden_rows.dtype)

def attend(query_matrix, key_value_rows, segments, alive_mask):
    input_rows = query_matrix.shape[0]
    query_groups = QUERY_HEADS // KEY_VALUE_HEADS
    quadruples = query_matrix.astype(jnp.float32).reshape(input_rows, KEY_VALUE_HEADS, query_groups, HEAD_SIZE)
    key_rows = key_value_rows[:, :KEY_VALUE_HEADS * HEAD_SIZE].astype(jnp.float32).reshape(input_rows, KEY_VALUE_HEADS, HEAD_SIZE)
    value_rows = key_value_rows[:, KEY_VALUE_HEADS * HEAD_SIZE:].astype(jnp.float32).reshape(input_rows, KEY_VALUE_HEADS, HEAD_SIZE)
    scores = jnp.einsum('tkgd,skd->kgts', quadruples, key_rows, precision=lax.Precision.HIGHEST) * HEAD_SIZE ** (-0.5)
    places = jnp.arange(input_rows)
    allowed = (segments[:, None] == segments[None, :]) & (places[None, :] <= places[:, None])
    weights = jnp.where(allowed[None, None], jnp.exp(scores), 0.0).astype(jnp.float32)
    totals = lax.optimization_barrier(jnp.sum(weights, axis=3))
    rounded = lax.optimization_barrier(weights.astype(key_value_rows.dtype)).astype(jnp.float32)
    mixed = jnp.einsum('kgts,skd->tkgd', rounded, value_rows, precision=lax.Precision.HIGHEST)
    mixed = mixed / jnp.transpose(totals, (2, 0, 1))[..., None]
    return jnp.where(alive_mask[:, None], mixed.reshape(input_rows, QUERY_HEADS * HEAD_SIZE), 0.0).astype(key_value_rows.dtype)

def reference(hidden, queries, source_table, norm_gain, key_value_weight, value_projection_bias, seq_lengths, seq_sources, dest_device, dest_slot, segment_ids):
    row_width = QUERY_HEADS * HEAD_SIZE
    hid_cols = hidden.reshape(N_DP, N_FSDP, DEVICE_TOKENS, MODEL_WIDTH).transpose(1, 0, 2, 3)
    qry_cols = queries.reshape(N_DP, N_FSDP, DEVICE_TOKENS, row_width).transpose(1, 0, 2, 3)
    seg_cols = segment_ids.reshape(N_DP, N_FSDP, DEVICE_TOKENS).transpose(1, 0, 2)
    complete_bias = jnp.concatenate([jnp.zeros((KEY_VALUE_HEADS * HEAD_SIZE,), jnp.float32), value_projection_bias.astype(jnp.float32)])

    def one_norm(hidden_rows, lengths, tags):
        return normalize(hidden_rows, source_table, norm_gain, lengths, tags)

    def single_device(packed):
        query_matrix, key_value_rows, segments, alive_mask = packed
        return attend(query_matrix, key_value_rows, segments, alive_mask)

    def per_column(packed):
        hid_col, qry_col, segment_column, lengths, tags, targets, offsets = packed
        normed = jax.vmap(one_norm)(hid_col, lengths.reshape(N_DP, SEQS), tags.reshape(N_DP, SEQS))
        flat = normed.reshape(N_DP * DEVICE_TOKENS, MODEL_WIDTH)
        src_index, alive_mask = source_rows(lengths, targets, offsets, DEVICE_TOKENS)
        moved = jnp.where(alive_mask[:, None], flat[src_index], 0)
        relocated_queries = jnp.where(alive_mask[:, None], qry_col.reshape(N_DP * DEVICE_TOKENS, row_width)[src_index], 0)
        key_value_rows = (jnp.dot(moved, key_value_weight, preferred_element_type=jnp.float32) + complete_bias[None, :]).astype(key_value_weight.dtype)
        return lax.map(single_device, (relocated_queries.reshape(N_DP, DEVICE_TOKENS, row_width), key_value_rows.reshape(N_DP, DEVICE_TOKENS, 2 * KEY_VALUE_HEADS * HEAD_SIZE), segment_column, alive_mask.reshape(N_DP, DEVICE_TOKENS)))
    result = lax.map(per_column, (hid_cols, qry_cols, seg_cols, seq_lengths, seq_sources, dest_device, dest_slot))
    return result.transpose(1, 0, 2, 3).reshape(TOKENS, row_width)
```

```python
import functools

import jax
import jax.numpy as jnp
from jax import lax
from jax.experimental import pallas as pl
from jax.experimental.pallas import tpu as pltpu
from jax.sharding import PartitionSpec as P

HEAD_SIZE = 128
QUERY_HEADS = 20
KEY_VALUE_HEADS = 4
SOURCES = 8
SEQS = 4


epsilon = 1e-06


def for_sending(shard):

    def short(part):
        return part.astype(jnp.bfloat16) if part.dtype == jnp.float32 else part

    return jax.tree.map(short, shard)


def source_rows(lengths, targets, offsets, input_rows):
    devices = lengths.shape[0] // SEQS
    grid = lengths.reshape(devices, SEQS)
    starts = (jnp.cumsum(grid, axis=1) - grid).reshape(-1)
    owners = jnp.arange(devices * SEQS) // SEQS
    src_base = owners * input_rows + starts
    dst_base = targets * input_rows + offsets
    places = jnp.arange(devices * input_rows)
    inside = (places[:, None] >= dst_base[None, :]) & (
        places[:, None] < (dst_base + lengths)[None, :]
    )
    shifts = jnp.sum(jnp.where(inside, (src_base - dst_base)[None, :], 0), axis=1)
    alive_mask = jnp.any(inside, axis=1)
    return (jnp.where(alive_mask, places + shifts, 0), alive_mask)


def normalize(hidden_rows, table, gain, lengths, tags):
    input_rows = hidden_rows.shape[0]
    starts = jnp.cumsum(lengths) - lengths
    places = jnp.arange(input_rows)
    inside = (places[:, None] >= starts[None, :]) & (places[:, None] < (starts + lengths)[None, :])
    kinds = jnp.arange(SOURCES)
    picks = jnp.any(inside[:, :, None] & (tags[None, :, None] == kinds[None, None, :]), axis=1)
    summed = hidden_rows.astype(jnp.float32) + jnp.dot(
        picks.astype(table.dtype), table, preferred_element_type=jnp.float32
    )
    scale = lax.rsqrt(jnp.mean(summed * summed, axis=1, keepdims=True) + epsilon)
    return (summed * scale * gain).astype(jnp.bfloat16)


def attend(query_matrix, key_value_rows, segments, alive_mask):
    input_rows = query_matrix.shape[0]
    query_groups = QUERY_HEADS // KEY_VALUE_HEADS
    quadruples = query_matrix.reshape(input_rows, KEY_VALUE_HEADS, query_groups, HEAD_SIZE)
    key_rows = key_value_rows[:, : KEY_VALUE_HEADS * HEAD_SIZE].reshape(
        input_rows, KEY_VALUE_HEADS, HEAD_SIZE
    )
    value_rows = key_value_rows[:, KEY_VALUE_HEADS * HEAD_SIZE :].reshape(
        input_rows, KEY_VALUE_HEADS, HEAD_SIZE
    )
    scores = jnp.einsum(
        "tkgd,skd->kgts", quadruples, key_rows, preferred_element_type=jnp.float32
    ) * HEAD_SIZE ** (-0.5)
    places = jnp.arange(input_rows)
    allowed = (segments[:, None] == segments[None, :]) & (places[None, :] <= places[:, None])
    weights = jnp.where(allowed[None, None], jnp.exp(scores), 0.0)
    totals = jnp.sum(weights, axis=3)
    mixed = jnp.einsum(
        "kgts,skd->tkgd",
        weights.astype(jnp.bfloat16),
        value_rows,
        preferred_element_type=jnp.float32,
    )
    mixed = mixed / jnp.transpose(totals, (2, 0, 1))[..., None]
    return jnp.where(
        alive_mask[:, None], mixed.reshape(input_rows, QUERY_HEADS * HEAD_SIZE), 0.0
    ).astype(jnp.bfloat16)


def relocate(blocks, src_index, alive_mask):
    spread = (
        lax.all_to_all(blocks[0], "dp", split_axis=1, concat_axis=0, tiled=True),
        lax.all_to_all(blocks[1], "dp", split_axis=1, concat_axis=0, tiled=True),
    )
    picked = tuple(
        (
            jnp.where(
                alive_mask[:, None], jnp.take(block, src_index, axis=0), jnp.zeros((), block.dtype)
            )
            for block in spread
        )
    )
    return jax.tree.map(
        lambda part, own: part.astype(own.dtype),
        lax.all_to_all(for_sending(picked), "dp", split_axis=0, concat_axis=1, tiled=True),
        picked,
    )


def project(token_block, key_value_weight, complete_bias):
    product = jnp.dot(
        token_block,
        lax.all_gather(key_value_weight, "fsdp", axis=1, tiled=True),
        preferred_element_type=jnp.float32,
    )
    total = product + complete_bias[None, :]
    return total.astype(jnp.bfloat16)


def body(
    hidden,
    queries,
    source_table,
    norm_gain,
    key_value_weight,
    value_projection_bias,
    seq_lengths,
    seq_sources,
    dest_device,
    dest_slot,
    segment_ids,
):
    input_rows = hidden.shape[0]
    lengths = seq_lengths[0]
    tags = seq_sources[0]
    targets = dest_device[0]
    offsets = dest_slot[0]
    position = lax.axis_index("dp")
    own_lengths = lax.dynamic_slice_in_dim(lengths, position * SEQS, SEQS)
    own_tags = lax.dynamic_slice_in_dim(tags, position * SEQS, SEQS)
    normed = normalize(hidden, source_table, norm_gain, own_lengths, own_tags)
    src_index, alive_mask = source_rows(lengths, targets, offsets, input_rows)
    own_living = lax.dynamic_slice_in_dim(alive_mask, position * input_rows, input_rows)
    complete_bias = jnp.concatenate(
        [jnp.zeros((KEY_VALUE_HEADS * HEAD_SIZE,), jnp.float32), value_projection_bias]
    )
    moved, relocated_queries = relocate((normed, queries), src_index, alive_mask)
    key_value_rows = project(moved, key_value_weight, complete_bias)
    return attend(relocated_queries, key_value_rows, segment_ids, own_living)


MESH_ID = pl.DeviceIdType.MESH
CHUNKS = 4


def fused_kernel(
    n_dp,
    lengths_ref,
    tags_ref,
    targets_ref,
    offsets_ref,
    hidden_ref,
    queries_ref,
    table_ref,
    gain_ref,
    weight_ref,
    bias_ref,
    seg_row_ref,
    seg_col_ref,
    out_ref,
    weight,
    rows_held,
    kv_own,
    kv_first,
    q_first,
    q_perm,
    kv_perm,
    q_last,
    kv_last,
    weight_sem,
    x_send,
    x_recv,
    c_send,
    c_recv,
    f_send,
    f_recv,
    q1_send,
    q1_recv,
    kv1_send,
    kv1_recv,
    q2_send,
    q2_recv,
    kv2_send,
    kv2_recv,
):
    rows = hidden_ref.shape[0]
    part = rows // CHUNKS
    every = n_dp * rows
    q_width = queries_ref.shape[1] // n_dp
    i = lax.axis_index("dp")
    f = lax.axis_index("fsdp")
    core_mate = f + 1 - 2 * lax.rem(f, 2)
    x_mate = lax.rem(f + 2, 4)
    diagonal = lax.rem(core_mate + 2, 4)
    holders = (f, core_mate, x_mate, diagonal)

    def remote(src, dst, send, recv, dp, fsdp):
        return pltpu.make_async_remote_copy(
            src_ref=src,
            dst_ref=dst,
            send_sem=send,
            recv_sem=recv,
            device_id={"dp": dp, "fsdp": fsdp},
            device_id_type=MESH_ID,
        )

    load_weight = pltpu.make_async_copy(weight_ref, weight, weight_sem)
    load_weight.start()
    barrier = pltpu.get_barrier_semaphore()
    for a in range(n_dp):
        for b in range(4):
            if a or b:
                pl.semaphore_signal(
                    barrier,
                    inc=1,
                    device_id={"dp": lax.rem(i + a, n_dp), "fsdp": lax.rem(f + b, 4)},
                    device_id_type=MESH_ID,
                )

    lengths = [lengths_ref[0, s] for s in range(n_dp * SEQS)]

    def norm_part(c):
        place = lax.broadcasted_iota(jnp.int32, (part, 1), 0) + c * part
        kind = jnp.full((part, 1), -1, jnp.int32)
        start = 0
        for s in range(SEQS):
            own_length = lengths_ref[0, i * SEQS + s]
            inside = (place >= start) & (place < start + own_length)
            kind = jnp.where(inside, tags_ref[0, i * SEQS + s], kind)
            start = start + own_length
        kinds = lax.broadcasted_iota(jnp.int32, (part, SOURCES), 1)
        picks = jnp.where(kinds == kind, 1.0, 0.0).astype(jnp.bfloat16)
        own = pl.ds(c * part, part)
        summed = hidden_ref[own, :].astype(jnp.float32) + jnp.dot(
            picks, table_ref[...], preferred_element_type=jnp.float32
        )
        scale = lax.rsqrt(jnp.mean(summed * summed, axis=1, keepdims=True) + epsilon)
        rows_held[0, own, :] = (summed * scale * gain_ref[...]).astype(jnp.bfloat16)

    def x_copy(c):
        own = pl.ds(c * part, part)
        return remote(
            rows_held.at[0, own], rows_held.at[2, own], x_send.at[c], x_recv.at[c], i, x_mate
        )

    def c_copy(c):
        own = pl.ds(c * part, part)
        return remote(
            rows_held.at[0, own], rows_held.at[1, own], c_send.at[c], c_recv.at[c], i, core_mate
        )

    def f_copy(c):
        own = pl.ds(c * part, part)
        return remote(
            rows_held.at[2, own], rows_held.at[3, own], f_send.at[c], f_recv.at[c], i, core_mate
        )

    def q1_copy(o):
        head = lax.rem(i + o, n_dp)
        cols = pl.ds(pl.multiple_of(head * q_width, 128), q_width)
        return remote(
            queries_ref.at[:, cols], q_first.at[i], q1_send.at[o], q1_recv.at[o], head, f
        )

    norm_part(0)
    pl.semaphore_wait(barrier, n_dp * 4 - 1)
    x_copy(0).start()
    c_copy(0).start()
    q1_own = pltpu.make_async_copy(
        queries_ref.at[:, pl.ds(pl.multiple_of(i * q_width, 128), q_width)],
        q_first.at[i],
        q1_recv.at[0],
    )
    q1_own.start()
    for o in range(1, n_dp):
        q1_copy(o).start()
    for c in range(1, CHUNKS):
        norm_part(c)
        x_copy(c).start()
        c_copy(c).start()

    kind_of_half = f // 2
    value_at = pl.multiple_of(lax.rem(f, 2) * 256, 256)
    bias = bias_ref[:, pl.ds(value_at, 256)] * kind_of_half.astype(jnp.float32)

    def project_part(slot, first, count):
        own = pl.ds(first, count)
        product = jnp.dot(
            rows_held[slot, own, :], weight[...], preferred_element_type=jnp.float32
        )
        kv = (product + bias).astype(jnp.bfloat16)
        for half in range(2):
            kv_own[slot, half, own, :] = kv[:, half * HEAD_SIZE : (half + 1) * HEAD_SIZE]

    def kv1_copy(slot, half, first, count):
        head = 2 * lax.rem(f, 2) + half
        landing = pl.ds(pl.multiple_of(i * rows + first, count), count)
        return remote(
            kv_own.at[slot, half, pl.ds(first, count)],
            kv_first.at[kind_of_half, landing],
            kv1_send.at[slot, half],
            kv1_recv.at[i, kind_of_half],
            head,
            holders[slot],
        )

    def send_kv(slot, first, count):
        for half in range(2):
            if slot == 0:
                head = 2 * lax.rem(f, 2) + half

                @pl.when(head != i)
                def _():
                    kv1_copy(slot, half, first, count).start()

                @pl.when(head == i)
                def _():
                    pltpu.make_async_copy(
                        kv_own.at[slot, half, pl.ds(first, count)],
                        kv_first.at[kind_of_half, pl.ds(pl.multiple_of(i * rows, rows), rows)],
                        kv1_recv.at[i, kind_of_half],
                    ).start()

            else:
                kv1_copy(slot, half, first, count).start()

    load_weight.wait()
    project_part(0, 0, rows)
    send_kv(0, 0, rows)

    lane = lax.broadcasted_iota(jnp.int32, (1, every), 1)
    target = jnp.full((1, every), -1, jnp.int32)
    for a in range(n_dp):
        start = a * rows
        for s in range(a * SEQS, (a + 1) * SEQS):
            inside = (lane >= start) & (lane < start + lengths[s])
            base = targets_ref[0, s] * rows + offsets_ref[0, s] - start
            target = jnp.where(inside, lane + base, target)
            start = start + lengths[s]

    def chosen(block):
        place = lax.broadcasted_iota(jnp.int32, (rows, every), 0) + block * rows
        return jnp.where(place == target, 1.0, 0.0).astype(jnp.bfloat16)

    def q2_copy(o):
        d = lax.rem(i + o, n_dp)
        return remote(
            q_perm.at[o], q_last.at[i], q2_send.at[o], q2_recv.at[o], d, f
        )

    def kv2_copy(o):
        d = lax.rem(i + o, n_dp)
        return remote(
            kv_perm.at[o], kv_last.at[i], kv2_send.at[o], kv2_recv.at[o], d, f
        )

    def move_queries():
        q1_own.wait()
        for o in range(1, n_dp):
            q1_copy(o).wait_recv()
        full = q_first[...].reshape(every, q_width)
        for o in (2, 3, 1, 0):
            moved = jnp.dot(
                chosen(lax.rem(i + o, n_dp)), full, preferred_element_type=jnp.float32
            ).astype(jnp.bfloat16)
            if o:
                q_perm[o] = moved
                q2_copy(o).start()
            else:
                q_last[i] = moved

    for c in range(CHUNKS):
        c_copy(c).wait_recv()
    project_part(1, 0, rows)
    send_kv(1, 0, rows)

    for c in range(CHUNKS):
        x_copy(c).wait_recv()
        f_copy(c).start()
        if c == CHUNKS // 2:
            move_queries()
        project_part(2, c * part, part)
        send_kv(2, c * part, part)
        f_copy(c).wait_recv()
        project_part(3, c * part, part)
        send_kv(3, c * part, part)

    for a in range(n_dp):
        for t in range(2):
            landing = kv_first.at[t, pl.ds(a * rows, rows)]
            remote(
                landing, landing, kv1_send.at[0, 0], kv1_recv.at[a, t], i, x_mate
            ).wait_recv()
    for o in (2, 3, 1, 0):
        pick = chosen(lax.rem(i + o, n_dp))
        for t in range(2):
            moved = jnp.dot(pick, kv_first[t], preferred_element_type=jnp.float32).astype(
                jnp.bfloat16
            )
            if o:
                kv_perm[o, t] = moved
            else:
                kv_last[i, t] = moved
        if o:
            kv2_copy(o).start()

    seg_col = seg_col_ref[...]
    row_at = lax.broadcasted_iota(jnp.int32, (rows, rows), 0)
    col_at = lax.broadcasted_iota(jnp.int32, (rows, rows), 1)
    allowed = (seg_col == seg_row_ref[...]) & (col_at <= row_at)
    alive = seg_col >= 0
    heads = QUERY_HEADS // KEY_VALUE_HEADS

    def attend_head(k):
        block = q_last[k]
        stacked = jnp.concatenate(
            [block[:, h * HEAD_SIZE : (h + 1) * HEAD_SIZE] for h in range(heads)], axis=0
        )
        scores = lax.dot_general(
            stacked,
            kv_last[k, 0],
            (((1,), (1,)), ((), ())),
            preferred_element_type=jnp.float32,
        ) * HEAD_SIZE ** (-0.5)
        scores = scores.reshape(heads, rows, rows)
        weights = jnp.where(allowed[None], jnp.exp(scores), 0.0)
        totals = jnp.sum(weights, axis=2, keepdims=True)
        mixed = jnp.dot(
            weights.astype(jnp.bfloat16).reshape(heads * rows, rows),
            kv_last[k, 1],
            preferred_element_type=jnp.float32,
        ).reshape(heads, rows, HEAD_SIZE)
        mixed = jnp.where(alive[None], mixed / totals, 0.0).astype(jnp.bfloat16)
        for h in range(heads):
            at = pl.multiple_of((k * heads + h) * HEAD_SIZE, HEAD_SIZE)
            out_ref[:, pl.ds(at, HEAD_SIZE)] = mixed[h]

    attend_head(i)
    for o in (1, 3, 2):
        q2_copy(o).wait_recv()
        kv2_copy(o).wait_recv()
        attend_head(lax.rem(i + n_dp - o, n_dp))

    for c in range(CHUNKS):
        x_copy(c).wait_send()
        c_copy(c).wait_send()
        f_copy(c).wait_send()
    for o in range(1, n_dp):
        q1_copy(o).wait_send()
        q2_copy(o).wait_send()
        kv2_copy(o).wait_send()
    for half in range(2):
        for slot in range(1, 4):
            kv1_copy(slot, half, 0, rows).wait_send()

        @pl.when(2 * lax.rem(f, 2) + half != i)
        def _():
            kv1_copy(0, half, 0, rows).wait_send()


def fused_body(
    n_dp,
    hidden,
    queries,
    source_table,
    norm_gain,
    key_value_weight,
    value_projection_bias,
    seq_lengths,
    seq_sources,
    dest_device,
    dest_slot,
    segment_ids,
):
    rows, model = hidden.shape
    q_width = queries.shape[1] // n_dp
    columns = key_value_weight.shape[1]
    every = n_dp * rows
    vmem = pl.BlockSpec(memory_space=pltpu.VMEM)
    smem = pl.BlockSpec(memory_space=pltpu.SMEM)
    anywhere = pl.BlockSpec(memory_space=pl.ANY)
    bf16 = jnp.bfloat16
    dma = pltpu.SemaphoreType.DMA
    return pl.pallas_call(
        functools.partial(fused_kernel, n_dp),
        out_shape=jax.ShapeDtypeStruct(queries.shape, bf16),
        in_specs=[smem] * 4 + [vmem, anywhere, vmem, vmem, anywhere, vmem, vmem, vmem],
        out_specs=vmem,
        scratch_shapes=[
            pltpu.VMEM((model, columns), bf16),
            pltpu.VMEM((4, rows, model), bf16),
            pltpu.VMEM((4, 2, rows, HEAD_SIZE), bf16),
            pltpu.VMEM((2, every, HEAD_SIZE), bf16),
            pltpu.VMEM((n_dp, rows, q_width), bf16),
            pltpu.VMEM((n_dp, rows, q_width), bf16),
            pltpu.VMEM((n_dp, 2, rows, HEAD_SIZE), bf16),
            pltpu.VMEM((n_dp, rows, q_width), bf16),
            pltpu.VMEM((n_dp, 2, rows, HEAD_SIZE), bf16),
            dma,
            dma((CHUNKS,)),
            dma((CHUNKS,)),
            dma((CHUNKS,)),
            dma((CHUNKS,)),
            dma((CHUNKS,)),
            dma((CHUNKS,)),
            dma((n_dp,)),
            dma((n_dp,)),
            dma((4, 2)),
            dma((n_dp, 2)),
            dma((n_dp,)),
            dma((n_dp,)),
            dma((n_dp,)),
            dma((n_dp,)),
        ],
        compiler_params=pltpu.CompilerParams(
            collective_id=0, has_side_effects=True, vmem_limit_bytes=40 * 2**20
        ),
        cost_estimate=pl.CostEstimate(
            flops=2 * 4 * rows * model * columns,
            bytes_accessed=8 * 2**20,
            transcendentals=QUERY_HEADS * rows * rows,
        ),
    )(
        seq_lengths,
        seq_sources,
        dest_device,
        dest_slot,
        hidden,
        queries,
        source_table,
        norm_gain[None, :],
        key_value_weight,
        value_projection_bias[None, :],
        segment_ids[None, :],
        segment_ids[:, None],
    )


def solution(mesh):
    placed = (
        P(("groups", "dp", "fsdp"), None),
        P(("groups", "dp", "fsdp"), None),
        P(),
        P(),
        P(None, "fsdp"),
        P(),
        P(("groups", "fsdp"), None),
        P(("groups", "fsdp"), None),
        P(("groups", "fsdp"), None),
        P(("groups", "fsdp"), None),
        P(("groups", "dp", "fsdp")),
    )
    n_dp = mesh.shape["dp"]
    heads_fit = n_dp == KEY_VALUE_HEADS and mesh.shape["fsdp"] == 4
    return jax.shard_map(
        functools.partial(fused_body, n_dp) if heads_fit else body,
        mesh=mesh,
        in_specs=placed,
        out_specs=P(("groups", "dp", "fsdp"), None),
        check_vma=False,
    )
```

```python
import functools

import jax
import jax.numpy as jnp
from jax import lax
from jax.experimental import pallas as pl
from jax.experimental.pallas import tpu as pltpu
from jax.sharding import PartitionSpec as P

HEAD_SIZE = 128
QUERY_HEADS = 20
KEY_VALUE_HEADS = 4
SOURCES = 8
SEQS = 4


epsilon = 1e-06


def for_sending(shard):

    def short(part):
        return part.astype(jnp.bfloat16) if part.dtype == jnp.float32 else part

    return jax.tree.map(short, shard)


def source_rows(lengths, targets, offsets, input_rows):
    devices = lengths.shape[0] // SEQS
    grid = lengths.reshape(devices, SEQS)
    starts = (jnp.cumsum(grid, axis=1) - grid).reshape(-1)
    owners = jnp.arange(devices * SEQS) // SEQS
    src_base = owners * input_rows + starts
    dst_base = targets * input_rows + offsets
    places = jnp.arange(devices * input_rows)
    inside = (places[:, None] >= dst_base[None, :]) & (
        places[:, None] < (dst_base + lengths)[None, :]
    )
    shifts = jnp.sum(jnp.where(inside, (src_base - dst_base)[None, :], 0), axis=1)
    alive_mask = jnp.any(inside, axis=1)
    return (jnp.where(alive_mask, places + shifts, 0), alive_mask)


def normalize(hidden_rows, table, gain, lengths, tags):
    input_rows = hidden_rows.shape[0]
    starts = jnp.cumsum(lengths) - lengths
    places = jnp.arange(input_rows)
    inside = (places[:, None] >= starts[None, :]) & (places[:, None] < (starts + lengths)[None, :])
    kinds = jnp.arange(SOURCES)
    picks = jnp.any(inside[:, :, None] & (tags[None, :, None] == kinds[None, None, :]), axis=1)
    summed = hidden_rows.astype(jnp.float32) + jnp.dot(
        picks.astype(table.dtype), table, preferred_element_type=jnp.float32
    )
    scale = lax.rsqrt(jnp.mean(summed * summed, axis=1, keepdims=True) + epsilon)
    return (summed * scale * gain).astype(jnp.bfloat16)


def attend(query_matrix, key_value_rows, segments, alive_mask):
    input_rows = query_matrix.shape[0]
    query_groups = QUERY_HEADS // KEY_VALUE_HEADS
    quadruples = query_matrix.reshape(input_rows, KEY_VALUE_HEADS, query_groups, HEAD_SIZE)
    key_rows = key_value_rows[:, : KEY_VALUE_HEADS * HEAD_SIZE].reshape(
        input_rows, KEY_VALUE_HEADS, HEAD_SIZE
    )
    value_rows = key_value_rows[:, KEY_VALUE_HEADS * HEAD_SIZE :].reshape(
        input_rows, KEY_VALUE_HEADS, HEAD_SIZE
    )
    scores = jnp.einsum(
        "tkgd,skd->kgts", quadruples, key_rows, preferred_element_type=jnp.float32
    ) * HEAD_SIZE ** (-0.5)
    places = jnp.arange(input_rows)
    allowed = (segments[:, None] == segments[None, :]) & (places[None, :] <= places[:, None])
    weights = jnp.where(allowed[None, None], jnp.exp(scores), 0.0)
    totals = jnp.sum(weights, axis=3)
    mixed = jnp.einsum(
        "kgts,skd->tkgd",
        weights.astype(jnp.bfloat16),
        value_rows,
        preferred_element_type=jnp.float32,
    )
    mixed = mixed / jnp.transpose(totals, (2, 0, 1))[..., None]
    return jnp.where(
        alive_mask[:, None], mixed.reshape(input_rows, QUERY_HEADS * HEAD_SIZE), 0.0
    ).astype(jnp.bfloat16)


def relocate(blocks, src_index, alive_mask):
    spread = (
        lax.all_to_all(blocks[0], "dp", split_axis=1, concat_axis=0, tiled=True),
        lax.all_to_all(blocks[1], "dp", split_axis=1, concat_axis=0, tiled=True),
    )
    picked = tuple(
        (
            jnp.where(
                alive_mask[:, None], jnp.take(block, src_index, axis=0), jnp.zeros((), block.dtype)
            )
            for block in spread
        )
    )
    return jax.tree.map(
        lambda part, own: part.astype(own.dtype),
        lax.all_to_all(for_sending(picked), "dp", split_axis=0, concat_axis=1, tiled=True),
        picked,
    )


def project(token_block, key_value_weight, complete_bias):
    product = jnp.dot(
        token_block,
        lax.all_gather(key_value_weight, "fsdp", axis=1, tiled=True),
        preferred_element_type=jnp.float32,
    )
    total = product + complete_bias[None, :]
    return total.astype(jnp.bfloat16)


def body(
    hidden,
    queries,
    source_table,
    norm_gain,
    key_value_weight,
    value_projection_bias,
    seq_lengths,
    seq_sources,
    dest_device,
    dest_slot,
    segment_ids,
):
    input_rows = hidden.shape[0]
    lengths = seq_lengths[0]
    tags = seq_sources[0]
    targets = dest_device[0]
    offsets = dest_slot[0]
    position = lax.axis_index("dp")
    own_lengths = lax.dynamic_slice_in_dim(lengths, position * SEQS, SEQS)
    own_tags = lax.dynamic_slice_in_dim(tags, position * SEQS, SEQS)
    normed = normalize(hidden, source_table, norm_gain, own_lengths, own_tags)
    src_index, alive_mask = source_rows(lengths, targets, offsets, input_rows)
    own_living = lax.dynamic_slice_in_dim(alive_mask, position * input_rows, input_rows)
    complete_bias = jnp.concatenate(
        [jnp.zeros((KEY_VALUE_HEADS * HEAD_SIZE,), jnp.float32), value_projection_bias]
    )
    moved, relocated_queries = relocate((normed, queries), src_index, alive_mask)
    key_value_rows = project(moved, key_value_weight, complete_bias)
    return attend(relocated_queries, key_value_rows, segment_ids, own_living)


MESH_ID = pl.DeviceIdType.MESH
CHUNKS = 4
VMEM_BYTES = 60 * 2**20


def fused_kernel(
    n_dp,
    lengths_ref,
    tags_ref,
    targets_ref,
    offsets_ref,
    hidden_ref,
    queries_ref,
    table_ref,
    gain_ref,
    weight_ref,
    bias_ref,
    seg_row_ref,
    out_ref,
    weight,
    rows_held,
    kv_own,
    kv_first,
    q_first,
    q_perm,
    kv_perm,
    q_last,
    kv_last,
    weight_sem,
    x_send,
    x_recv,
    c_send,
    c_recv,
    f_send,
    f_recv,
    q1_send,
    q1_recv,
    kv1_send,
    kv1_recv,
    q2_send,
    q2_recv,
    kv2_send,
    kv2_recv,
):
    rows = hidden_ref.shape[0]
    part = rows // CHUNKS
    every = n_dp * rows
    q_width = queries_ref.shape[1] // n_dp
    i = lax.axis_index("dp")
    f = lax.axis_index("fsdp")
    core_mate = f + 1 - 2 * lax.rem(f, 2)
    x_mate = lax.rem(f + 2, 4)
    diagonal = lax.rem(core_mate + 2, 4)
    holders = (f, core_mate, x_mate, diagonal)

    def remote(src, dst, send, recv, dp, fsdp):
        return pltpu.make_async_remote_copy(
            src_ref=src,
            dst_ref=dst,
            send_sem=send,
            recv_sem=recv,
            device_id={"dp": dp, "fsdp": fsdp},
            device_id_type=MESH_ID,
        )

    load_weight = pltpu.make_async_copy(weight_ref, weight, weight_sem)
    load_weight.start()
    barrier = pltpu.get_barrier_semaphore()
    for a in range(n_dp):
        for b in range(4):
            if a or b:
                pl.semaphore_signal(
                    barrier,
                    inc=1,
                    device_id={"dp": lax.rem(i + a, n_dp), "fsdp": lax.rem(f + b, 4)},
                    device_id_type=MESH_ID,
                )

    lengths = [lengths_ref[0, s] for s in range(n_dp * SEQS)]

    def norm_part(c):
        place = lax.broadcasted_iota(jnp.int32, (part, 1), 0) + c * part
        kind = jnp.full((part, 1), -1, jnp.int32)
        start = 0
        for s in range(SEQS):
            own_length = lengths_ref[0, i * SEQS + s]
            inside = (place >= start) & (place < start + own_length)
            kind = jnp.where(inside, tags_ref[0, i * SEQS + s], kind)
            start = start + own_length
        kinds = lax.broadcasted_iota(jnp.int32, (part, SOURCES), 1)
        picks = jnp.where(kinds == kind, 1.0, 0.0).astype(jnp.bfloat16)
        own = pl.ds(c * part, part)
        summed = hidden_ref[own, :].astype(jnp.float32) + jnp.dot(
            picks, table_ref[...], preferred_element_type=jnp.float32
        )
        scale = lax.rsqrt(jnp.mean(summed * summed, axis=1, keepdims=True) + epsilon)
        rows_held[0, own, :] = (summed * scale * gain_ref[...]).astype(jnp.bfloat16)

    def x_copy(c):
        own = pl.ds(c * part, part)
        return remote(
            rows_held.at[0, own], rows_held.at[2, own], x_send.at[c], x_recv.at[c], i, x_mate
        )

    def c_copy(c):
        own = pl.ds(c * part, part)
        return remote(
            rows_held.at[0, own], rows_held.at[1, own], c_send.at[c], c_recv.at[c], i, core_mate
        )

    def f_copy(c):
        own = pl.ds(c * part, part)
        return remote(
            rows_held.at[2, own], rows_held.at[3, own], f_send.at[c], f_recv.at[c], i, core_mate
        )

    first_width = (q_width // HEAD_SIZE + 1) // 2 * HEAD_SIZE
    pieces = ((0, first_width), (first_width, q_width - first_width))

    def q1_source(head, piece):
        at, width = pieces[piece]
        return queries_ref.at[:, pl.ds(pl.multiple_of(head * q_width + at, HEAD_SIZE), width)]

    def q1_copy(o, piece):
        head = lax.rem(i + o, n_dp)
        return remote(
            q1_source(head, piece),
            q_first.at[i, :, pl.ds(*pieces[piece])],
            q1_send.at[o, piece],
            q1_recv.at[o, piece],
            head,
            f,
        )

    def q1_own(piece):
        return pltpu.make_async_copy(
            q1_source(i, piece),
            q_first.at[i, :, pl.ds(*pieces[piece])],
            q1_recv.at[0, piece],
        )

    pl.semaphore_wait(barrier, n_dp * 4 - 1)
    for piece in range(2):
        for o in (2, 3, 1):
            q1_copy(o, piece).start()
        q1_own(piece).start()
    for c in range(CHUNKS):
        norm_part(c)
        x_copy(c).start()
        c_copy(c).start()

    kind_of_half = f // 2
    value_at = pl.multiple_of(lax.rem(f, 2) * 256, 256)
    bias = bias_ref[:, pl.ds(value_at, 256)] * kind_of_half.astype(jnp.float32)

    def project_part(slot, first, count):
        own = pl.ds(first, count)
        product = jnp.dot(
            rows_held[slot, own, :], weight[...], preferred_element_type=jnp.float32
        )
        kv = (product + bias).astype(jnp.bfloat16)
        for half in range(2):
            kv_own[slot, half, own, :] = kv[:, half * HEAD_SIZE : (half + 1) * HEAD_SIZE]

    def kv1_copy(slot, half, first, count):
        head = 2 * lax.rem(f, 2) + half
        landing = pl.ds(pl.multiple_of(i * rows + first, count), count)
        return remote(
            kv_own.at[slot, half, pl.ds(first, count)],
            kv_first.at[kind_of_half, landing],
            kv1_send.at[slot, half],
            kv1_recv.at[i, kind_of_half],
            head,
            holders[slot],
        )

    def send_kv(slot, first, count):
        for half in range(2):
            if slot == 0:
                head = 2 * lax.rem(f, 2) + half

                @pl.when(head != i)
                def _():
                    kv1_copy(slot, half, first, count).start()

                @pl.when(head == i)
                def _():
                    pltpu.make_async_copy(
                        kv_own.at[slot, half, pl.ds(first, count)],
                        kv_first.at[kind_of_half, pl.ds(pl.multiple_of(i * rows, rows), rows)],
                        kv1_recv.at[i, kind_of_half],
                    ).start()

            else:
                kv1_copy(slot, half, first, count).start()

    load_weight.wait()
    project_part(0, 0, rows)
    send_kv(0, 0, rows)

    lane = lax.broadcasted_iota(jnp.int32, (1, every), 1)
    target = jnp.full((1, every), -1, jnp.int32)
    for a in range(n_dp):
        start = a * rows
        for s in range(a * SEQS, (a + 1) * SEQS):
            inside = (lane >= start) & (lane < start + lengths[s])
            base = targets_ref[0, s] * rows + offsets_ref[0, s] - start
            target = jnp.where(inside, lane + base, target)
            start = start + lengths[s]

    def chosen(block):
        place = lax.broadcasted_iota(jnp.int32, (rows, every), 0) + block * rows
        return jnp.where(place == target, 1.0, 0.0).astype(jnp.bfloat16)

    def q2_copy(o, piece):
        d = lax.rem(i + o, n_dp)
        cols = pl.ds(*pieces[piece])
        return remote(
            q_perm.at[o, :, cols],
            q_last.at[i, :, cols],
            q2_send.at[o, piece],
            q2_recv.at[o, piece],
            d,
            f,
        )

    def kv2_copy(o):
        d = lax.rem(i + o, n_dp)
        return remote(
            kv_perm.at[o], kv_last.at[i], kv2_send.at[o], kv2_recv.at[o], d, f
        )

    def move_queries(piece):
        q1_own(piece).wait()
        for o in range(1, n_dp):
            q1_copy(o, piece).wait_recv()
        at, width = pieces[piece]
        cols = pl.ds(at, width)
        full = q_first[:, :, cols].reshape(every, width)
        for o in (2, 3, 1, 0):
            moved = jnp.dot(
                chosen(lax.rem(i + o, n_dp)), full, preferred_element_type=jnp.float32
            ).astype(jnp.bfloat16)
            if o:
                q_perm[o, :, cols] = moved
                q2_copy(o, piece).start()
            else:
                q_last[i, :, cols] = moved

    for c in range(CHUNKS):
        c_copy(c).wait_recv()
    project_part(1, 0, rows)
    send_kv(1, 0, rows)

    for c in range(CHUNKS):
        x_copy(c).wait_recv()
        f_copy(c).start()
        project_part(2, c * part, part)
        send_kv(2, c * part, part)
        f_copy(c).wait_recv()
        project_part(3, c * part, part)
        send_kv(3, c * part, part)
        if c < 2:
            move_queries(c)

    for a in range(n_dp):
        for t in range(2):
            landing = kv_first.at[t, pl.ds(a * rows, rows)]
            remote(
                landing, landing, kv1_send.at[0, 0], kv1_recv.at[a, t], i, x_mate
            ).wait_recv()
    for o in (2, 3, 1, 0):
        pick = chosen(lax.rem(i + o, n_dp))
        for t in range(2):
            moved = jnp.dot(pick, kv_first[t], preferred_element_type=jnp.float32).astype(
                jnp.bfloat16
            )
            if o:
                kv_perm[o, t] = moved
            else:
                kv_last[i, t] = moved
        if o:
            kv2_copy(o).start()

    seg_row = jnp.broadcast_to(seg_row_ref[...].astype(jnp.float32), (rows, rows))
    seg_col = jnp.transpose(seg_row)
    row_at = lax.broadcasted_iota(jnp.int32, (rows, rows), 0)
    col_at = lax.broadcasted_iota(jnp.int32, (rows, rows), 1)
    allowed = (seg_col == seg_row) & (col_at <= row_at)
    alive = seg_col >= 0
    heads = QUERY_HEADS // KEY_VALUE_HEADS

    def attend_head(k):
        block = q_last[k]
        stacked = jnp.concatenate(
            [block[:, h * HEAD_SIZE : (h + 1) * HEAD_SIZE] for h in range(heads)], axis=0
        )
        scores = lax.dot_general(
            stacked,
            kv_last[k, 0],
            (((1,), (1,)), ((), ())),
            preferred_element_type=jnp.float32,
        ) * HEAD_SIZE ** (-0.5)
        scores = scores.reshape(heads, rows, rows)
        weights = jnp.where(allowed[None], jnp.exp(scores), 0.0)
        totals = jnp.sum(weights, axis=2, keepdims=True)
        mixed = jnp.dot(
            weights.astype(jnp.bfloat16).reshape(heads * rows, rows),
            kv_last[k, 1],
            preferred_element_type=jnp.float32,
        ).reshape(heads, rows, HEAD_SIZE)
        mixed = jnp.where(alive[None], mixed / totals, 0.0).astype(jnp.bfloat16)
        for h in range(heads):
            at = pl.multiple_of((k * heads + h) * HEAD_SIZE, HEAD_SIZE)
            out_ref[:, pl.ds(at, HEAD_SIZE)] = mixed[h]

    attend_head(i)
    for o in (1, 3, 2):
        for piece in range(2):
            q2_copy(o, piece).wait_recv()
        kv2_copy(o).wait_recv()
        attend_head(lax.rem(i + n_dp - o, n_dp))

    for c in range(CHUNKS):
        x_copy(c).wait_send()
        c_copy(c).wait_send()
        f_copy(c).wait_send()
    for o in range(1, n_dp):
        for piece in range(2):
            q1_copy(o, piece).wait_send()
            q2_copy(o, piece).wait_send()
        kv2_copy(o).wait_send()
    for half in range(2):
        for slot in range(1, 4):
            kv1_copy(slot, half, 0, rows).wait_send()

        @pl.when(2 * lax.rem(f, 2) + half != i)
        def _():
            kv1_copy(0, half, 0, rows).wait_send()


def fused_body(
    n_dp,
    hidden,
    queries,
    source_table,
    norm_gain,
    key_value_weight,
    value_projection_bias,
    seq_lengths,
    seq_sources,
    dest_device,
    dest_slot,
    segment_ids,
):
    rows, model = hidden.shape
    q_width = queries.shape[1] // n_dp
    columns = key_value_weight.shape[1]
    every = n_dp * rows
    vmem = pl.BlockSpec(memory_space=pltpu.VMEM)
    smem = pl.BlockSpec(memory_space=pltpu.SMEM)
    anywhere = pl.BlockSpec(memory_space=pl.ANY)
    bf16 = jnp.bfloat16
    dma = pltpu.SemaphoreType.DMA
    return pl.pallas_call(
        functools.partial(fused_kernel, n_dp),
        out_shape=jax.ShapeDtypeStruct(queries.shape, bf16),
        in_specs=[smem] * 4 + [vmem, anywhere, vmem, vmem, anywhere, vmem, vmem],
        out_specs=vmem,
        scratch_shapes=[
            pltpu.VMEM((model, columns), bf16),
            pltpu.VMEM((4, rows, model), bf16),
            pltpu.VMEM((4, 2, rows, HEAD_SIZE), bf16),
            pltpu.VMEM((2, every, HEAD_SIZE), bf16),
            pltpu.VMEM((n_dp, rows, q_width), bf16),
            pltpu.VMEM((n_dp, rows, q_width), bf16),
            pltpu.VMEM((n_dp, 2, rows, HEAD_SIZE), bf16),
            pltpu.VMEM((n_dp, rows, q_width), bf16),
            pltpu.VMEM((n_dp, 2, rows, HEAD_SIZE), bf16),
            dma,
            dma((CHUNKS,)),
            dma((CHUNKS,)),
            dma((CHUNKS,)),
            dma((CHUNKS,)),
            dma((CHUNKS,)),
            dma((CHUNKS,)),
            dma((n_dp, 2)),
            dma((n_dp, 2)),
            dma((4, 2)),
            dma((n_dp, 2)),
            dma((n_dp, 2)),
            dma((n_dp, 2)),
            dma((n_dp,)),
            dma((n_dp,)),
        ],
        compiler_params=pltpu.CompilerParams(
            collective_id=0, has_side_effects=True, vmem_limit_bytes=VMEM_BYTES
        ),
        cost_estimate=pl.CostEstimate(
            flops=2 * 4 * rows * model * columns,
            bytes_accessed=8 * 2**20,
            transcendentals=QUERY_HEADS * rows * rows,
        ),
    )(
        seq_lengths,
        seq_sources,
        dest_device,
        dest_slot,
        hidden,
        queries,
        source_table,
        norm_gain[None, :],
        key_value_weight,
        value_projection_bias[None, :],
        segment_ids[None, :],
    )


def solution(mesh):
    placed = (
        P(("groups", "dp", "fsdp"), None),
        P(("groups", "dp", "fsdp"), None),
        P(),
        P(),
        P(None, "fsdp"),
        P(),
        P(("groups", "fsdp"), None),
        P(("groups", "fsdp"), None),
        P(("groups", "fsdp"), None),
        P(("groups", "fsdp"), None),
        P(("groups", "dp", "fsdp")),
    )
    n_dp = mesh.shape["dp"]
    heads_fit = n_dp == KEY_VALUE_HEADS and mesh.shape["fsdp"] == 4
    return jax.shard_map(
        functools.partial(fused_body, n_dp) if heads_fit else body,
        mesh=mesh,
        in_specs=placed,
        out_specs=P(("groups", "dp", "fsdp"), None),
        check_vma=False,
    )
```

```python
import functools

import jax
import jax.numpy as jnp
from jax import lax
from jax.experimental import pallas as pl
from jax.experimental.pallas import tpu as pltpu
from jax.sharding import PartitionSpec as P

HEAD_SIZE = 128
QUERY_HEADS = 20
KEY_VALUE_HEADS = 4
SOURCES = 8
SEQS = 4


epsilon = 1e-06


def for_sending(shard):

    def short(part):
        return part.astype(jnp.bfloat16) if part.dtype == jnp.float32 else part

    return jax.tree.map(short, shard)


def source_rows(lengths, targets, offsets, input_rows):
    devices = lengths.shape[0] // SEQS
    grid = lengths.reshape(devices, SEQS)
    starts = (jnp.cumsum(grid, axis=1) - grid).reshape(-1)
    owners = jnp.arange(devices * SEQS) // SEQS
    src_base = owners * input_rows + starts
    dst_base = targets * input_rows + offsets
    places = jnp.arange(devices * input_rows)
    inside = (places[:, None] >= dst_base[None, :]) & (
        places[:, None] < (dst_base + lengths)[None, :]
    )
    shifts = jnp.sum(jnp.where(inside, (src_base - dst_base)[None, :], 0), axis=1)
    alive_mask = jnp.any(inside, axis=1)
    return (jnp.where(alive_mask, places + shifts, 0), alive_mask)


def normalize(hidden_rows, table, gain, lengths, tags):
    input_rows = hidden_rows.shape[0]
    starts = jnp.cumsum(lengths) - lengths
    places = jnp.arange(input_rows)
    inside = (places[:, None] >= starts[None, :]) & (places[:, None] < (starts + lengths)[None, :])
    kinds = jnp.arange(SOURCES)
    picks = jnp.any(inside[:, :, None] & (tags[None, :, None] == kinds[None, None, :]), axis=1)
    summed = hidden_rows.astype(jnp.float32) + jnp.dot(
        picks.astype(table.dtype), table, preferred_element_type=jnp.float32
    )
    scale = lax.rsqrt(jnp.mean(summed * summed, axis=1, keepdims=True) + epsilon)
    return (summed * scale * gain).astype(jnp.bfloat16)


def attend(query_matrix, key_value_rows, segments, alive_mask):
    input_rows = query_matrix.shape[0]
    query_groups = QUERY_HEADS // KEY_VALUE_HEADS
    quadruples = query_matrix.reshape(input_rows, KEY_VALUE_HEADS, query_groups, HEAD_SIZE)
    key_rows = key_value_rows[:, : KEY_VALUE_HEADS * HEAD_SIZE].reshape(
        input_rows, KEY_VALUE_HEADS, HEAD_SIZE
    )
    value_rows = key_value_rows[:, KEY_VALUE_HEADS * HEAD_SIZE :].reshape(
        input_rows, KEY_VALUE_HEADS, HEAD_SIZE
    )
    scores = jnp.einsum(
        "tkgd,skd->kgts", quadruples, key_rows, preferred_element_type=jnp.float32
    ) * HEAD_SIZE ** (-0.5)
    places = jnp.arange(input_rows)
    allowed = (segments[:, None] == segments[None, :]) & (places[None, :] <= places[:, None])
    weights = jnp.where(allowed[None, None], jnp.exp(scores), 0.0)
    totals = jnp.sum(weights, axis=3)
    mixed = jnp.einsum(
        "kgts,skd->tkgd",
        weights.astype(jnp.bfloat16),
        value_rows,
        preferred_element_type=jnp.float32,
    )
    mixed = mixed / jnp.transpose(totals, (2, 0, 1))[..., None]
    return jnp.where(
        alive_mask[:, None], mixed.reshape(input_rows, QUERY_HEADS * HEAD_SIZE), 0.0
    ).astype(jnp.bfloat16)


def relocate(blocks, src_index, alive_mask):
    spread = (
        lax.all_to_all(blocks[0], "dp", split_axis=1, concat_axis=0, tiled=True),
        lax.all_to_all(blocks[1], "dp", split_axis=1, concat_axis=0, tiled=True),
    )
    picked = tuple(
        (
            jnp.where(
                alive_mask[:, None], jnp.take(block, src_index, axis=0), jnp.zeros((), block.dtype)
            )
            for block in spread
        )
    )
    return jax.tree.map(
        lambda part, own: part.astype(own.dtype),
        lax.all_to_all(for_sending(picked), "dp", split_axis=0, concat_axis=1, tiled=True),
        picked,
    )


def project(token_block, key_value_weight, complete_bias):
    product = jnp.dot(
        token_block,
        lax.all_gather(key_value_weight, "fsdp", axis=1, tiled=True),
        preferred_element_type=jnp.float32,
    )
    total = product + complete_bias[None, :]
    return total.astype(jnp.bfloat16)


def body(
    hidden,
    queries,
    source_table,
    norm_gain,
    key_value_weight,
    value_projection_bias,
    seq_lengths,
    seq_sources,
    dest_device,
    dest_slot,
    segment_ids,
):
    input_rows = hidden.shape[0]
    lengths = seq_lengths[0]
    tags = seq_sources[0]
    targets = dest_device[0]
    offsets = dest_slot[0]
    position = lax.axis_index("dp")
    own_lengths = lax.dynamic_slice_in_dim(lengths, position * SEQS, SEQS)
    own_tags = lax.dynamic_slice_in_dim(tags, position * SEQS, SEQS)
    normed = normalize(hidden, source_table, norm_gain, own_lengths, own_tags)
    src_index, alive_mask = source_rows(lengths, targets, offsets, input_rows)
    own_living = lax.dynamic_slice_in_dim(alive_mask, position * input_rows, input_rows)
    complete_bias = jnp.concatenate(
        [jnp.zeros((KEY_VALUE_HEADS * HEAD_SIZE,), jnp.float32), value_projection_bias]
    )
    moved, relocated_queries = relocate((normed, queries), src_index, alive_mask)
    key_value_rows = project(moved, key_value_weight, complete_bias)
    return attend(relocated_queries, key_value_rows, segment_ids, own_living)


MESH_ID = pl.DeviceIdType.MESH
CHUNKS = 4
EARLY_CHUNK = 2
VMEM_BYTES = 60 * 2**20


def fused_kernel(
    n_dp,
    lengths_ref,
    tags_ref,
    targets_ref,
    offsets_ref,
    hidden_from,
    queries_ref,
    table_ref,
    gain_ref,
    weight_ref,
    bias_ref,
    seg_row_ref,
    out_ref,
    hidden_ref,
    weight,
    rows_held,
    kv_own,
    kv_first,
    q_first,
    q_perm,
    kv_perm,
    q_last,
    kv_last,
    hidden_sem,
    weight_sem,
    x_send,
    x_recv,
    c_send,
    c_recv,
    f_send,
    f_recv,
    q1_send,
    q1_recv,
    kv1_send,
    kv1_recv,
    q2_send,
    q2_recv,
    kv2_send,
    kv2_recv,
):
    rows = hidden_from.shape[0]
    part = rows // CHUNKS
    every = n_dp * rows
    q_width = queries_ref.shape[1] // n_dp
    i = lax.axis_index("dp")
    f = lax.axis_index("fsdp")
    core_mate = f + 1 - 2 * lax.rem(f, 2)
    x_mate = lax.rem(f + 2, 4)
    diagonal = lax.rem(core_mate + 2, 4)
    holders = (f, core_mate, x_mate, diagonal)

    def remote(src, dst, send, recv, dp, fsdp):
        return pltpu.make_async_remote_copy(
            src_ref=src,
            dst_ref=dst,
            send_sem=send,
            recv_sem=recv,
            device_id={"dp": dp, "fsdp": fsdp},
            device_id_type=MESH_ID,
        )

    load_weight = pltpu.make_async_copy(weight_ref, weight, weight_sem)
    load_hidden = pltpu.make_async_copy(hidden_from, hidden_ref, hidden_sem)
    load_hidden.start()
    barrier = pltpu.get_barrier_semaphore()
    for a in range(n_dp):
        for b in range(4):
            if a or b:
                pl.semaphore_signal(
                    barrier,
                    inc=1,
                    device_id={"dp": lax.rem(i + a, n_dp), "fsdp": lax.rem(f + b, 4)},
                    device_id_type=MESH_ID,
                )

    lengths = [lengths_ref[0, s] for s in range(n_dp * SEQS)]

    def norm_part(c):
        place = lax.broadcasted_iota(jnp.int32, (part, 1), 0) + c * part
        kind = jnp.full((part, 1), -1, jnp.int32)
        start = 0
        for s in range(SEQS):
            own_length = lengths_ref[0, i * SEQS + s]
            inside = (place >= start) & (place < start + own_length)
            kind = jnp.where(inside, tags_ref[0, i * SEQS + s], kind)
            start = start + own_length
        kinds = lax.broadcasted_iota(jnp.int32, (part, SOURCES), 1)
        picks = jnp.where(kinds == kind, 1.0, 0.0).astype(jnp.bfloat16)
        own = pl.ds(c * part, part)
        summed = hidden_ref[own, :].astype(jnp.float32) + jnp.dot(
            picks, table_ref[...], preferred_element_type=jnp.float32
        )
        scale = lax.rsqrt(jnp.mean(summed * summed, axis=1, keepdims=True) + epsilon)
        rows_held[0, own, :] = (summed * scale * gain_ref[...]).astype(jnp.bfloat16)

    def x_copy(c):
        own = pl.ds(c * part, part)
        return remote(
            rows_held.at[0, own], rows_held.at[2, own], x_send.at[c], x_recv.at[c], i, x_mate
        )

    def c_copy(c):
        own = pl.ds(c * part, part)
        return remote(
            rows_held.at[0, own], rows_held.at[1, own], c_send.at[c], c_recv.at[c], i, core_mate
        )

    def f_copy(c):
        own = pl.ds(c * part, part)
        return remote(
            rows_held.at[2, own], rows_held.at[3, own], f_send.at[c], f_recv.at[c], i, core_mate
        )

    first_width = (q_width // HEAD_SIZE + 1) // 2 * HEAD_SIZE
    pieces = ((0, first_width), (first_width, q_width - first_width))

    def q1_source(head, piece):
        at, width = pieces[piece]
        return queries_ref.at[:, pl.ds(pl.multiple_of(head * q_width + at, HEAD_SIZE), width)]

    def q1_copy(o, piece):
        head = lax.rem(i + o, n_dp)
        return remote(
            q1_source(head, piece),
            q_first.at[i, :, pl.ds(*pieces[piece])],
            q1_send.at[o, piece],
            q1_recv.at[o, piece],
            head,
            f,
        )

    def q1_own(piece):
        return pltpu.make_async_copy(
            q1_source(i, piece),
            q_first.at[i, :, pl.ds(*pieces[piece])],
            q1_recv.at[0, piece],
        )

    load_weight.start()
    pl.semaphore_wait(barrier, n_dp * 4 - 1)
    for piece in range(2):
        for o in (2, 3, 1):
            q1_copy(o, piece).start()
        q1_own(piece).start()
    load_hidden.wait()
    for c in range(CHUNKS):
        norm_part(c)
        x_copy(c).start()
        c_copy(c).start()

    kind_of_half = f // 2
    value_at = pl.multiple_of(lax.rem(f, 2) * 256, 256)
    bias = bias_ref[:, pl.ds(value_at, 256)] * kind_of_half.astype(jnp.float32)

    def project_part(slot, first, count):
        own = pl.ds(first, count)
        product = jnp.dot(
            rows_held[slot, own, :], weight[...], preferred_element_type=jnp.float32
        )
        kv = (product + bias).astype(jnp.bfloat16)
        for half in range(2):
            kv_own[slot, half, own, :] = kv[:, half * HEAD_SIZE : (half + 1) * HEAD_SIZE]

    def kv1_copy(slot, half, first, count):
        head = 2 * lax.rem(f, 2) + half
        landing = pl.ds(pl.multiple_of(i * rows + first, count), count)
        return remote(
            kv_own.at[slot, half, pl.ds(first, count)],
            kv_first.at[kind_of_half, landing],
            kv1_send.at[slot, half],
            kv1_recv.at[i, kind_of_half],
            head,
            holders[slot],
        )

    def send_kv(slot, first, count):
        for half in range(2):
            if slot == 0:
                head = 2 * lax.rem(f, 2) + half

                @pl.when(head != i)
                def _():
                    kv1_copy(slot, half, first, count).start()

                @pl.when(head == i)
                def _():
                    pltpu.make_async_copy(
                        kv_own.at[slot, half, pl.ds(first, count)],
                        kv_first.at[kind_of_half, pl.ds(pl.multiple_of(i * rows, rows), rows)],
                        kv1_recv.at[i, kind_of_half],
                    ).start()

            else:
                kv1_copy(slot, half, first, count).start()

    load_weight.wait()
    project_part(0, 0, rows)
    send_kv(0, 0, rows)

    lane = lax.broadcasted_iota(jnp.int32, (1, every), 1)
    target = jnp.full((1, every), -1, jnp.int32)
    for a in range(n_dp):
        start = a * rows
        for s in range(a * SEQS, (a + 1) * SEQS):
            inside = (lane >= start) & (lane < start + lengths[s])
            base = targets_ref[0, s] * rows + offsets_ref[0, s] - start
            target = jnp.where(inside, lane + base, target)
            start = start + lengths[s]

    def chosen(block):
        place = lax.broadcasted_iota(jnp.int32, (rows, every), 0) + block * rows
        return jnp.where(place == target, 1.0, 0.0).astype(jnp.bfloat16)

    def q2_copy(o, piece):
        d = lax.rem(i + o, n_dp)
        cols = pl.ds(*pieces[piece])
        return remote(
            q_perm.at[o, :, cols],
            q_last.at[i, :, cols],
            q2_send.at[o, piece],
            q2_recv.at[o, piece],
            d,
            f,
        )

    def kv2_copy(o, t):
        d = lax.rem(i + o, n_dp)
        return remote(
            kv_perm.at[o, t],
            kv_last.at[i, t],
            kv2_send.at[o, t],
            kv2_recv.at[o, t],
            d,
            f,
        )

    def move_keys_or_values(t):
        for a in range(n_dp):
            landing = kv_first.at[t, pl.ds(a * rows, rows)]
            remote(
                landing, landing, kv1_send.at[0, 0], kv1_recv.at[a, t], i, x_mate
            ).wait_recv()
        full = kv_first[t]
        for o in (2, 3, 1, 0):
            moved = jnp.dot(
                chosen(lax.rem(i + o, n_dp)), full, preferred_element_type=jnp.float32
            ).astype(jnp.bfloat16)
            if o:
                kv_perm[o, t] = moved
                kv2_copy(o, t).start()
            else:
                kv_last[i, t] = moved

    def move_queries(piece):
        q1_own(piece).wait()
        for o in range(1, n_dp):
            q1_copy(o, piece).wait_recv()
        at, width = pieces[piece]
        cols = pl.ds(at, width)
        full = q_first[:, :, cols].reshape(every, width)
        for o in (2, 3, 1, 0):
            moved = jnp.dot(
                chosen(lax.rem(i + o, n_dp)), full, preferred_element_type=jnp.float32
            ).astype(jnp.bfloat16)
            if o:
                q_perm[o, :, cols] = moved
                q2_copy(o, piece).start()
            else:
                q_last[i, :, cols] = moved

    for c in range(CHUNKS):
        c_copy(c).wait_recv()
    project_part(1, 0, rows)
    send_kv(1, 0, rows)

    for c in range(CHUNKS):
        x_copy(c).wait_recv()
        f_copy(c).start()
        project_part(2, c * part, part)
        send_kv(2, c * part, part)
        f_copy(c).wait_recv()
        project_part(3, c * part, part)
        send_kv(3, c * part, part)
        if c < 2:
            move_queries(c)
        if c == EARLY_CHUNK:
            move_keys_or_values(kind_of_half)

    move_keys_or_values(1 - kind_of_half)

    seg_row = jnp.broadcast_to(seg_row_ref[...].astype(jnp.float32), (rows, rows))
    seg_col = jnp.transpose(seg_row)
    row_at = lax.broadcasted_iota(jnp.int32, (rows, rows), 0)
    col_at = lax.broadcasted_iota(jnp.int32, (rows, rows), 1)
    allowed = (seg_col == seg_row) & (col_at <= row_at)
    heads = QUERY_HEADS // KEY_VALUE_HEADS

    def attend_head(k):
        block = q_last[k]
        stacked = jnp.concatenate(
            [block[:, h * HEAD_SIZE : (h + 1) * HEAD_SIZE] for h in range(heads)], axis=0
        )
        scores = lax.dot_general(
            stacked,
            kv_last[k, 0],
            (((1,), (1,)), ((), ())),
            preferred_element_type=jnp.float32,
        ) * HEAD_SIZE ** (-0.5)
        scores = scores.reshape(heads, rows, rows)
        weights = jnp.where(allowed[None], jnp.exp(scores), 0.0)
        totals = jnp.sum(weights, axis=2, keepdims=True)
        mixed = jnp.dot(
            weights.astype(jnp.bfloat16).reshape(heads * rows, rows),
            kv_last[k, 1],
            preferred_element_type=jnp.float32,
        ).reshape(heads, rows, HEAD_SIZE)
        mixed = (mixed / totals).astype(jnp.bfloat16)
        for h in range(heads):
            at = pl.multiple_of((k * heads + h) * HEAD_SIZE, HEAD_SIZE)
            out_ref[:, pl.ds(at, HEAD_SIZE)] = mixed[h]

    attend_head(i)
    for o in (1, 3, 2):
        for piece in range(2):
            q2_copy(o, piece).wait_recv()
        for t in range(2):
            kv2_copy(o, t).wait_recv()
        attend_head(lax.rem(i + n_dp - o, n_dp))

    for c in range(CHUNKS):
        x_copy(c).wait_send()
        c_copy(c).wait_send()
        f_copy(c).wait_send()
    for o in range(1, n_dp):
        for piece in range(2):
            q1_copy(o, piece).wait_send()
            q2_copy(o, piece).wait_send()
        for t in range(2):
            kv2_copy(o, t).wait_send()
    for half in range(2):
        for slot in range(1, 4):
            kv1_copy(slot, half, 0, rows).wait_send()

        @pl.when(2 * lax.rem(f, 2) + half != i)
        def _():
            kv1_copy(0, half, 0, rows).wait_send()


def fused_body(
    n_dp,
    hidden,
    queries,
    source_table,
    norm_gain,
    key_value_weight,
    value_projection_bias,
    seq_lengths,
    seq_sources,
    dest_device,
    dest_slot,
    segment_ids,
):
    rows, model = hidden.shape
    q_width = queries.shape[1] // n_dp
    columns = key_value_weight.shape[1]
    every = n_dp * rows
    vmem = pl.BlockSpec(memory_space=pltpu.VMEM)
    smem = pl.BlockSpec(memory_space=pltpu.SMEM)
    anywhere = pl.BlockSpec(memory_space=pl.ANY)
    bf16 = jnp.bfloat16
    dma = pltpu.SemaphoreType.DMA
    attended = pl.pallas_call(
        functools.partial(fused_kernel, n_dp),
        out_shape=jax.ShapeDtypeStruct(queries.shape, bf16),
        in_specs=[smem] * 4 + [anywhere, anywhere, vmem, vmem, anywhere, vmem, vmem],
        out_specs=vmem,
        scratch_shapes=[
            pltpu.VMEM((rows, model), bf16),
            pltpu.VMEM((model, columns), bf16),
            pltpu.VMEM((4, rows, model), bf16),
            pltpu.VMEM((4, 2, rows, HEAD_SIZE), bf16),
            pltpu.VMEM((2, every, HEAD_SIZE), bf16),
            pltpu.VMEM((n_dp, rows, q_width), bf16),
            pltpu.VMEM((n_dp, rows, q_width), bf16),
            pltpu.VMEM((n_dp, 2, rows, HEAD_SIZE), bf16),
            pltpu.VMEM((n_dp, rows, q_width), bf16),
            pltpu.VMEM((n_dp, 2, rows, HEAD_SIZE), bf16),
            dma,
            dma,
            dma((CHUNKS,)),
            dma((CHUNKS,)),
            dma((CHUNKS,)),
            dma((CHUNKS,)),
            dma((CHUNKS,)),
            dma((CHUNKS,)),
            dma((n_dp, 2)),
            dma((n_dp, 2)),
            dma((4, 2)),
            dma((n_dp, 2)),
            dma((n_dp, 2)),
            dma((n_dp, 2)),
            dma((n_dp, 2)),
            dma((n_dp, 2)),
        ],
        compiler_params=pltpu.CompilerParams(
            collective_id=0, has_side_effects=True, vmem_limit_bytes=VMEM_BYTES
        ),
        cost_estimate=pl.CostEstimate(
            flops=2 * 4 * rows * model * columns,
            bytes_accessed=8 * 2**20,
            transcendentals=QUERY_HEADS * rows * rows,
        ),
    )(
        seq_lengths,
        seq_sources,
        dest_device,
        dest_slot,
        hidden,
        queries,
        source_table,
        norm_gain[None, :],
        key_value_weight,
        value_projection_bias[None, :],
        segment_ids[None, :],
    )
    return jnp.where(segment_ids[:, None] >= 0, attended, jnp.zeros((), bf16))


def solution(mesh):
    placed = (
        P(("groups", "dp", "fsdp"), None),
        P(("groups", "dp", "fsdp"), None),
        P(),
        P(),
        P(None, "fsdp"),
        P(),
        P(("groups", "fsdp"), None),
        P(("groups", "fsdp"), None),
        P(("groups", "fsdp"), None),
        P(("groups", "fsdp"), None),
        P(("groups", "dp", "fsdp")),
    )
    n_dp = mesh.shape["dp"]
    heads_fit = n_dp == KEY_VALUE_HEADS and mesh.shape["fsdp"] == 4
    return jax.shard_map(
        functools.partial(fused_body, n_dp) if heads_fit else body,
        mesh=mesh,
        in_specs=placed,
        out_specs=P(("groups", "dp", "fsdp"), None),
        check_vma=False,
    )
```

```python
import functools

import jax
import jax.numpy as jnp
from jax import lax
from jax.experimental import pallas as pl
from jax.experimental.pallas import tpu as pltpu
from jax.sharding import PartitionSpec as P

HEAD_SIZE = 128
QUERY_HEADS = 20
KEY_VALUE_HEADS = 4
SOURCES = 8
SEQS = 4


epsilon = 1e-06


def for_sending(shard):

    def short(part):
        return part.astype(jnp.bfloat16) if part.dtype == jnp.float32 else part

    return jax.tree.map(short, shard)


def source_rows(lengths, targets, offsets, input_rows):
    devices = lengths.shape[0] // SEQS
    grid = lengths.reshape(devices, SEQS)
    starts = (jnp.cumsum(grid, axis=1) - grid).reshape(-1)
    owners = jnp.arange(devices * SEQS) // SEQS
    src_base = owners * input_rows + starts
    dst_base = targets * input_rows + offsets
    places = jnp.arange(devices * input_rows)
    inside = (places[:, None] >= dst_base[None, :]) & (
        places[:, None] < (dst_base + lengths)[None, :]
    )
    shifts = jnp.sum(jnp.where(inside, (src_base - dst_base)[None, :], 0), axis=1)
    alive_mask = jnp.any(inside, axis=1)
    return (jnp.where(alive_mask, places + shifts, 0), alive_mask)


def normalize(hidden_rows, table, gain, lengths, tags):
    input_rows = hidden_rows.shape[0]
    starts = jnp.cumsum(lengths) - lengths
    places = jnp.arange(input_rows)
    inside = (places[:, None] >= starts[None, :]) & (places[:, None] < (starts + lengths)[None, :])
    kinds = jnp.arange(SOURCES)
    picks = jnp.any(inside[:, :, None] & (tags[None, :, None] == kinds[None, None, :]), axis=1)
    summed = hidden_rows.astype(jnp.float32) + jnp.dot(
        picks.astype(table.dtype), table, preferred_element_type=jnp.float32
    )
    scale = lax.rsqrt(jnp.mean(summed * summed, axis=1, keepdims=True) + epsilon)
    return (summed * scale * gain).astype(jnp.bfloat16)


def attend(query_matrix, key_value_rows, segments, alive_mask):
    input_rows = query_matrix.shape[0]
    query_groups = QUERY_HEADS // KEY_VALUE_HEADS
    quadruples = query_matrix.reshape(input_rows, KEY_VALUE_HEADS, query_groups, HEAD_SIZE)
    key_rows = key_value_rows[:, : KEY_VALUE_HEADS * HEAD_SIZE].reshape(
        input_rows, KEY_VALUE_HEADS, HEAD_SIZE
    )
    value_rows = key_value_rows[:, KEY_VALUE_HEADS * HEAD_SIZE :].reshape(
        input_rows, KEY_VALUE_HEADS, HEAD_SIZE
    )
    scores = jnp.einsum(
        "tkgd,skd->kgts", quadruples, key_rows, preferred_element_type=jnp.float32
    ) * HEAD_SIZE ** (-0.5)
    places = jnp.arange(input_rows)
    allowed = (segments[:, None] == segments[None, :]) & (places[None, :] <= places[:, None])
    weights = jnp.where(allowed[None, None], jnp.exp(scores), 0.0)
    totals = jnp.sum(weights, axis=3)
    mixed = jnp.einsum(
        "kgts,skd->tkgd",
        weights.astype(jnp.bfloat16),
        value_rows,
        preferred_element_type=jnp.float32,
    )
    mixed = mixed / jnp.transpose(totals, (2, 0, 1))[..., None]
    return jnp.where(
        alive_mask[:, None], mixed.reshape(input_rows, QUERY_HEADS * HEAD_SIZE), 0.0
    ).astype(jnp.bfloat16)


def relocate(blocks, src_index, alive_mask):
    spread = (
        lax.all_to_all(blocks[0], "dp", split_axis=1, concat_axis=0, tiled=True),
        lax.all_to_all(blocks[1], "dp", split_axis=1, concat_axis=0, tiled=True),
    )
    picked = tuple(
        (
            jnp.where(
                alive_mask[:, None], jnp.take(block, src_index, axis=0), jnp.zeros((), block.dtype)
            )
            for block in spread
        )
    )
    return jax.tree.map(
        lambda part, own: part.astype(own.dtype),
        lax.all_to_all(for_sending(picked), "dp", split_axis=0, concat_axis=1, tiled=True),
        picked,
    )


def project(token_block, key_value_weight, complete_bias):
    product = jnp.dot(
        token_block,
        lax.all_gather(key_value_weight, "fsdp", axis=1, tiled=True),
        preferred_element_type=jnp.float32,
    )
    total = product + complete_bias[None, :]
    return total.astype(jnp.bfloat16)


def body(
    hidden,
    queries,
    source_table,
    norm_gain,
    key_value_weight,
    value_projection_bias,
    seq_lengths,
    seq_sources,
    dest_device,
    dest_slot,
    segment_ids,
):
    input_rows = hidden.shape[0]
    lengths = seq_lengths[0]
    tags = seq_sources[0]
    targets = dest_device[0]
    offsets = dest_slot[0]
    position = lax.axis_index("dp")
    own_lengths = lax.dynamic_slice_in_dim(lengths, position * SEQS, SEQS)
    own_tags = lax.dynamic_slice_in_dim(tags, position * SEQS, SEQS)
    normed = normalize(hidden, source_table, norm_gain, own_lengths, own_tags)
    src_index, alive_mask = source_rows(lengths, targets, offsets, input_rows)
    own_living = lax.dynamic_slice_in_dim(alive_mask, position * input_rows, input_rows)
    complete_bias = jnp.concatenate(
        [jnp.zeros((KEY_VALUE_HEADS * HEAD_SIZE,), jnp.float32), value_projection_bias]
    )
    moved, relocated_queries = relocate((normed, queries), src_index, alive_mask)
    key_value_rows = project(moved, key_value_weight, complete_bias)
    return attend(relocated_queries, key_value_rows, segment_ids, own_living)


MESH_ID = pl.DeviceIdType.MESH
CHUNKS = 4
EARLY_CHUNK = 2
VMEM_BYTES = 60 * 2**20


def fused_kernel(
    n_dp,
    lengths_ref,
    tags_ref,
    targets_ref,
    offsets_ref,
    hidden_from,
    queries_ref,
    table_ref,
    gain_ref,
    weight_ref,
    bias_ref,
    seg_row_ref,
    out_ref,
    hidden_ref,
    weight,
    rows_held,
    kv_own,
    kv_first,
    q_first,
    q_perm,
    kv_perm,
    q_last,
    kv_last,
    hidden_sem,
    weight_sem,
    x_send,
    x_recv,
    c_send,
    c_recv,
    f_send,
    f_recv,
    q1_send,
    q1_recv,
    kv1_send,
    kv1_recv,
    q2_send,
    q2_recv,
    kv2_send,
    kv2_recv,
):
    rows = hidden_from.shape[0]
    part = rows // CHUNKS
    every = n_dp * rows
    q_width = queries_ref.shape[1] // n_dp
    i = lax.axis_index("dp")
    f = lax.axis_index("fsdp")
    core_mate = f + 1 - 2 * lax.rem(f, 2)
    x_mate = lax.rem(f + 2, 4)
    diagonal = lax.rem(core_mate + 2, 4)
    holders = (f, core_mate, x_mate, diagonal)

    def remote(src, dst, send, recv, dp, fsdp):
        return pltpu.make_async_remote_copy(
            src_ref=src,
            dst_ref=dst,
            send_sem=send,
            recv_sem=recv,
            device_id={"dp": dp, "fsdp": fsdp},
            device_id_type=MESH_ID,
        )

    load_weight = pltpu.make_async_copy(weight_ref, weight, weight_sem)
    load_hidden = pltpu.make_async_copy(hidden_from, hidden_ref, hidden_sem)
    load_hidden.start()
    barrier = pltpu.get_barrier_semaphore()
    for a in range(n_dp):
        for b in range(4):
            if a or b:
                pl.semaphore_signal(
                    barrier,
                    inc=1,
                    device_id={"dp": lax.rem(i + a, n_dp), "fsdp": lax.rem(f + b, 4)},
                    device_id_type=MESH_ID,
                )

    lengths = [lengths_ref[0, s] for s in range(n_dp * SEQS)]

    def norm_part(c):
        place = lax.broadcasted_iota(jnp.int32, (part, 1), 0) + c * part
        kind = jnp.full((part, 1), -1, jnp.int32)
        start = 0
        for s in range(SEQS):
            own_length = lengths_ref[0, i * SEQS + s]
            inside = (place >= start) & (place < start + own_length)
            kind = jnp.where(inside, tags_ref[0, i * SEQS + s], kind)
            start = start + own_length
        kinds = lax.broadcasted_iota(jnp.int32, (part, SOURCES), 1)
        picks = jnp.where(kinds == kind, 1.0, 0.0).astype(jnp.bfloat16)
        own = pl.ds(c * part, part)
        summed = hidden_ref[own, :].astype(jnp.float32) + jnp.dot(
            picks, table_ref[...], preferred_element_type=jnp.float32
        )
        scale = lax.rsqrt(jnp.mean(summed * summed, axis=1, keepdims=True) + epsilon)
        rows_held[0, own, :] = (summed * scale * gain_ref[...]).astype(jnp.bfloat16)

    def x_copy(c):
        own = pl.ds(c * part, part)
        return remote(
            rows_held.at[0, own], rows_held.at[2, own], x_send.at[c], x_recv.at[c], i, x_mate
        )

    def c_copy(c):
        own = pl.ds(c * part, part)
        return remote(
            rows_held.at[0, own], rows_held.at[1, own], c_send.at[c], c_recv.at[c], i, core_mate
        )

    def f_copy(c):
        own = pl.ds(c * part, part)
        return remote(
            rows_held.at[2, own], rows_held.at[3, own], f_send.at[c], f_recv.at[c], i, core_mate
        )

    first_width = (q_width // HEAD_SIZE + 1) // 2 * HEAD_SIZE
    pieces = ((0, first_width), (first_width, q_width - first_width))

    def q1_source(head, piece):
        at, width = pieces[piece]
        return queries_ref.at[:, pl.ds(pl.multiple_of(head * q_width + at, HEAD_SIZE), width)]

    def q1_copy(o, piece):
        head = lax.rem(i + o, n_dp)
        return remote(
            q1_source(head, piece),
            q_first.at[i, :, pl.ds(*pieces[piece])],
            q1_send.at[o, piece],
            q1_recv.at[o, piece],
            head,
            f,
        )

    def q1_own(piece):
        return pltpu.make_async_copy(
            q1_source(i, piece),
            q_first.at[i, :, pl.ds(*pieces[piece])],
            q1_recv.at[0, piece],
        )

    load_weight.start()
    pl.semaphore_wait(barrier, n_dp * 4 - 1)
    for piece in range(2):
        for o in (2, 3, 1):
            q1_copy(o, piece).start()
        q1_own(piece).start()
    load_hidden.wait()
    for c in range(CHUNKS):
        norm_part(c)
        x_copy(c).start()
        c_copy(c).start()

    kind_of_half = f // 2
    value_at = pl.multiple_of(lax.rem(f, 2) * 256, 256)
    bias = bias_ref[:, pl.ds(value_at, 256)] * kind_of_half.astype(jnp.float32)

    def project_part(slot, first, count):
        own = pl.ds(first, count)
        product = jnp.dot(
            rows_held[slot, own, :], weight[...], preferred_element_type=jnp.float32
        )
        kv = (product + bias).astype(jnp.bfloat16)
        for half in range(2):
            kv_own[slot, half, own, :] = kv[:, half * HEAD_SIZE : (half + 1) * HEAD_SIZE]

    def project_pair(first, count):
        own = pl.ds(first, count)
        both = jnp.concatenate([rows_held[2, own, :], rows_held[3, own, :]], axis=0)
        product = jnp.dot(both, weight[...], preferred_element_type=jnp.float32)
        kv = (product + bias).astype(jnp.bfloat16)
        for slot in range(2):
            for half in range(2):
                kv_own[2 + slot, half, own, :] = kv[
                    slot * count : (slot + 1) * count,
                    half * HEAD_SIZE : (half + 1) * HEAD_SIZE,
                ]

    def kv1_copy(slot, half, first, count):
        head = 2 * lax.rem(f, 2) + half
        landing = pl.ds(pl.multiple_of(i * rows + first, count), count)
        return remote(
            kv_own.at[slot, half, pl.ds(first, count)],
            kv_first.at[kind_of_half, landing],
            kv1_send.at[slot, half],
            kv1_recv.at[i, kind_of_half],
            head,
            holders[slot],
        )

    def send_kv(slot, first, count):
        for half in range(2):
            if slot == 0:
                head = 2 * lax.rem(f, 2) + half

                @pl.when(head != i)
                def _():
                    kv1_copy(slot, half, first, count).start()

                @pl.when(head == i)
                def _():
                    pltpu.make_async_copy(
                        kv_own.at[slot, half, pl.ds(first, count)],
                        kv_first.at[kind_of_half, pl.ds(pl.multiple_of(i * rows, rows), rows)],
                        kv1_recv.at[i, kind_of_half],
                    ).start()

            else:
                kv1_copy(slot, half, first, count).start()

    load_weight.wait()
    project_part(0, 0, rows)
    send_kv(0, 0, rows)

    lane = lax.broadcasted_iota(jnp.int32, (1, every), 1)
    target = jnp.full((1, every), -1, jnp.int32)
    for a in range(n_dp):
        start = a * rows
        for s in range(a * SEQS, (a + 1) * SEQS):
            inside = (lane >= start) & (lane < start + lengths[s])
            base = targets_ref[0, s] * rows + offsets_ref[0, s] - start
            target = jnp.where(inside, lane + base, target)
            start = start + lengths[s]

    def chosen(block):
        place = lax.broadcasted_iota(jnp.int32, (rows, every), 0) + block * rows
        return jnp.where(place == target, 1.0, 0.0).astype(jnp.bfloat16)

    def q2_copy(o, piece):
        d = lax.rem(i + o, n_dp)
        cols = pl.ds(*pieces[piece])
        return remote(
            q_perm.at[o, :, cols],
            q_last.at[i, :, cols],
            q2_send.at[o, piece],
            q2_recv.at[o, piece],
            d,
            f,
        )

    def kv2_copy(o, t):
        d = lax.rem(i + o, n_dp)
        return remote(
            kv_perm.at[o, t],
            kv_last.at[i, t],
            kv2_send.at[o, t],
            kv2_recv.at[o, t],
            d,
            f,
        )

    def move_keys_or_values(t):
        for a in range(n_dp):
            landing = kv_first.at[t, pl.ds(a * rows, rows)]
            remote(
                landing, landing, kv1_send.at[0, 0], kv1_recv.at[a, t], i, x_mate
            ).wait_recv()
        full = kv_first[t]
        for o in (2, 3, 1, 0):
            moved = jnp.dot(
                chosen(lax.rem(i + o, n_dp)), full, preferred_element_type=jnp.float32
            ).astype(jnp.bfloat16)
            if o:
                kv_perm[o, t] = moved
                kv2_copy(o, t).start()
            else:
                kv_last[i, t] = moved

    def move_queries(piece):
        q1_own(piece).wait()
        for o in range(1, n_dp):
            q1_copy(o, piece).wait_recv()
        at, width = pieces[piece]
        cols = pl.ds(at, width)
        full = q_first[:, :, cols].reshape(every, width)
        for o in (2, 3, 1, 0):
            moved = jnp.dot(
                chosen(lax.rem(i + o, n_dp)), full, preferred_element_type=jnp.float32
            ).astype(jnp.bfloat16)
            if o:
                q_perm[o, :, cols] = moved
                q2_copy(o, piece).start()
            else:
                q_last[i, :, cols] = moved

    for c in range(CHUNKS):
        c_copy(c).wait_recv()
    project_part(1, 0, rows)
    send_kv(1, 0, rows)

    for c in range(CHUNKS):
        x_copy(c).wait_recv()
        f_copy(c).start()
        f_copy(c).wait_recv()
        project_pair(c * part, part)
        send_kv(2, c * part, part)
        send_kv(3, c * part, part)
        if c < 2:
            move_queries(c)
        if c == EARLY_CHUNK:
            move_keys_or_values(kind_of_half)

    move_keys_or_values(1 - kind_of_half)

    seg_row = jnp.broadcast_to(seg_row_ref[...].astype(jnp.float32), (rows, rows))
    seg_col = jnp.transpose(seg_row)
    row_at = lax.broadcasted_iota(jnp.int32, (rows, rows), 0)
    col_at = lax.broadcasted_iota(jnp.int32, (rows, rows), 1)
    allowed = (seg_col == seg_row) & (col_at <= row_at)
    alive = seg_col >= 0
    heads = QUERY_HEADS // KEY_VALUE_HEADS

    def attend_head(k):
        block = q_last[k]
        stacked = jnp.concatenate(
            [block[:, h * HEAD_SIZE : (h + 1) * HEAD_SIZE] for h in range(heads)], axis=0
        )
        scores = lax.dot_general(
            stacked,
            kv_last[k, 0],
            (((1,), (1,)), ((), ())),
            preferred_element_type=jnp.float32,
        ) * HEAD_SIZE ** (-0.5)
        scores = scores.reshape(heads, rows, rows)
        weights = jnp.where(allowed[None], jnp.exp(scores), 0.0)
        totals = jnp.sum(weights, axis=2, keepdims=True)
        mixed = jnp.dot(
            weights.astype(jnp.bfloat16).reshape(heads * rows, rows),
            kv_last[k, 1],
            preferred_element_type=jnp.float32,
        ).reshape(heads, rows, HEAD_SIZE)
        mixed = jnp.where(alive[None], mixed / totals, 0.0).astype(jnp.bfloat16)
        for h in range(heads):
            at = pl.multiple_of((k * heads + h) * HEAD_SIZE, HEAD_SIZE)
            out_ref[:, pl.ds(at, HEAD_SIZE)] = mixed[h]

    attend_head(i)
    for o in (1, 3, 2):
        for piece in range(2):
            q2_copy(o, piece).wait_recv()
        for t in range(2):
            kv2_copy(o, t).wait_recv()
        attend_head(lax.rem(i + n_dp - o, n_dp))

    for c in range(CHUNKS):
        x_copy(c).wait_send()
        c_copy(c).wait_send()
        f_copy(c).wait_send()
    for o in range(1, n_dp):
        for piece in range(2):
            q1_copy(o, piece).wait_send()
            q2_copy(o, piece).wait_send()
        for t in range(2):
            kv2_copy(o, t).wait_send()
    for half in range(2):
        for slot in range(1, 4):
            kv1_copy(slot, half, 0, rows).wait_send()

        @pl.when(2 * lax.rem(f, 2) + half != i)
        def _():
            kv1_copy(0, half, 0, rows).wait_send()


def fused_body(
    n_dp,
    hidden,
    queries,
    source_table,
    norm_gain,
    key_value_weight,
    value_projection_bias,
    seq_lengths,
    seq_sources,
    dest_device,
    dest_slot,
    segment_ids,
):
    rows, model = hidden.shape
    q_width = queries.shape[1] // n_dp
    columns = key_value_weight.shape[1]
    every = n_dp * rows
    vmem = pl.BlockSpec(memory_space=pltpu.VMEM)
    smem = pl.BlockSpec(memory_space=pltpu.SMEM)
    anywhere = pl.BlockSpec(memory_space=pl.ANY)
    bf16 = jnp.bfloat16
    dma = pltpu.SemaphoreType.DMA
    return pl.pallas_call(
        functools.partial(fused_kernel, n_dp),
        out_shape=jax.ShapeDtypeStruct(queries.shape, bf16),
        in_specs=[smem] * 4 + [anywhere, anywhere, vmem, vmem, anywhere, vmem, vmem],
        out_specs=vmem,
        scratch_shapes=[
            pltpu.VMEM((rows, model), bf16),
            pltpu.VMEM((model, columns), bf16),
            pltpu.VMEM((4, rows, model), bf16),
            pltpu.VMEM((4, 2, rows, HEAD_SIZE), bf16),
            pltpu.VMEM((2, every, HEAD_SIZE), bf16),
            pltpu.VMEM((n_dp, rows, q_width), bf16),
            pltpu.VMEM((n_dp, rows, q_width), bf16),
            pltpu.VMEM((n_dp, 2, rows, HEAD_SIZE), bf16),
            pltpu.VMEM((n_dp, rows, q_width), bf16),
            pltpu.VMEM((n_dp, 2, rows, HEAD_SIZE), bf16),
            dma,
            dma,
            dma((CHUNKS,)),
            dma((CHUNKS,)),
            dma((CHUNKS,)),
            dma((CHUNKS,)),
            dma((CHUNKS,)),
            dma((CHUNKS,)),
            dma((n_dp, 2)),
            dma((n_dp, 2)),
            dma((4, 2)),
            dma((n_dp, 2)),
            dma((n_dp, 2)),
            dma((n_dp, 2)),
            dma((n_dp, 2)),
            dma((n_dp, 2)),
        ],
        compiler_params=pltpu.CompilerParams(
            collective_id=0, has_side_effects=True, vmem_limit_bytes=VMEM_BYTES
        ),
        cost_estimate=pl.CostEstimate(
            flops=2 * 4 * rows * model * columns,
            bytes_accessed=8 * 2**20,
            transcendentals=QUERY_HEADS * rows * rows,
        ),
    )(
        seq_lengths,
        seq_sources,
        dest_device,
        dest_slot,
        hidden,
        queries,
        source_table,
        norm_gain[None, :],
        key_value_weight,
        value_projection_bias[None, :],
        segment_ids[None, :],
    )


def solution(mesh):
    placed = (
        P(("groups", "dp", "fsdp"), None),
        P(("groups", "dp", "fsdp"), None),
        P(),
        P(),
        P(None, "fsdp"),
        P(),
        P(("groups", "fsdp"), None),
        P(("groups", "fsdp"), None),
        P(("groups", "fsdp"), None),
        P(("groups", "fsdp"), None),
        P(("groups", "dp", "fsdp")),
    )
    n_dp = mesh.shape["dp"]
    heads_fit = n_dp == KEY_VALUE_HEADS and mesh.shape["fsdp"] == 4
    return jax.shard_map(
        functools.partial(fused_body, n_dp) if heads_fit else body,
        mesh=mesh,
        in_specs=placed,
        out_specs=P(("groups", "dp", "fsdp"), None),
        check_vma=False,
    )
```
